32 devices in a mesh: row: 4 (over y, core), col: 8 (over z, x).
Axes of the slice: x: 2, y: 2, z: 4, core: 2. Of those that a mesh axis runs over, the one named last changes fastest.
Arguments:
- parent_front: float32 [4, 4, 256, 2, 8, 256], P(None, 'row', None, None, 'col'), may hold values from -6 to 48, as said below
- child_tiles: bfloat16 [32, 16, 256, 256], P(('row', 'col')), may hold values from -6 to 6
- tile_target: int32 [32, 16, 2], replicated, may hold values from 0 to 15, as said below
Outputs:
- factored_front: float32 [4, 4, 256, 2, 8, 256], P(None, 'row', None, None, 'col')
The draws below stay inside these ranges and needn't reach their ends.
Inputs may be any that keep to these rules, and one draw needn't show every extreme that they name: The leading 6 * 256 rows and columns of parent_front form a symmetric matrix with diagonal entries in 32 to 48 and other entries of magnitude at most 30 / 1536. tile_target[d, s] is the parent tile (row, column) into which tile s of device d is added (device d is mesh row d // 8, column d % 8); rows are 6 or more. Parent tile (I, J) lives on mesh row I % 4, column J % 8. The 16 tiles of one device go to 16 different devices, and one device receives a tile from every device.
All inputs are finite; a program needn't handle non-finite values.
Results may differ from the reference program's by a relative error of at most 0.0003.
Values may be sent and summed in bfloat16 or wider, within the bound.
A program may use at most 192 MiB of HBM per device.

```python
import jax
import jax.numpy as jnp
from jax import lax

TILE = 256
PANELS = 6
LROWS = 4
PTILES = 16
LCOLS = 2
FRONT = 4096
STORED = 16
N_ROW = 4
N_COL = 8
DEVICES = 32


def draw_parent_front(key, part):
    key_base, key_raw, key_diag = jax.random.split(jax.random.fold_in(key, 5), 3)
    shape = (LROWS, N_ROW, TILE, LCOLS, N_COL, TILE)
    base = jnp.clip(jax.random.normal(key_base, shape, jnp.float32), -6.0, 6.0)
    order = PANELS * TILE
    bound = 30.0 / order
    raw = jax.random.uniform(key_raw, (order, order), jnp.float32, -bound, bound)
    symmetric = 0.5 * (raw + raw.T)
    diag = jax.random.uniform(key_diag, (order,), jnp.float32, 32.0, 48.0)
    identity = jnp.eye(order, dtype=jnp.float32)
    leading = symmetric * (1.0 - identity) + identity * diag[None, :]
    for first in range(PANELS):
        for second in range(PANELS):
            block = leading[first * TILE:(first + 1) * TILE, second * TILE:(second + 1) * TILE]
            base = base.at[first // N_ROW, first % N_ROW, :, second // N_COL, second % N_COL, :].set(block)
    return base


def draw_tile_target(key, part):
    busiest = jax.random.randint(jax.random.fold_in(key, 11), (), 0, DEVICES)
    keys = jax.random.split(jax.random.fold_in(key, 12), DEVICES)

    def one_device(device_key):
        key_perm, key_shuffle, key_rows, key_cols = jax.random.split(device_key, 4)
        others = jax.random.permutation(key_perm, DEVICES - 1).astype(jnp.int32)
        others = others + (others >= busiest).astype(jnp.int32)
        owners = jnp.concatenate([busiest.reshape(1).astype(jnp.int32), others[:STORED - 1]])
        owners = jax.random.permutation(key_shuffle, owners)
        owner_row = owners // N_COL
        owner_col = owners % N_COL
        lowest = jnp.maximum((PANELS - owner_row + N_ROW - 1) // N_ROW, 0).astype(jnp.int32)
        local_row = jax.random.randint(key_rows, (STORED,), lowest, LROWS)
        local_col = jax.random.randint(key_cols, (STORED,), 0, LCOLS)
        rows = owner_row + N_ROW * local_row
        cols = owner_col + N_COL * local_col
        return jnp.stack([rows, cols], axis=1).astype(jnp.int32)
    return jax.vmap(one_device)(keys)


def levels(own_key, dims, shards, smallest, high):
    loudness, own = 1.0, jax.random.fold_in(own_key, 6)
    for dim, shards_of in shards:
        heights = jnp.exp(jax.random.uniform(jax.random.fold_in(own, dim), (shards_of,), jnp.float32, smallest / len(shards), high / len(shards)))
        loudness = loudness * jnp.repeat(heights, dims[dim] // shards_of).reshape([-1 if axis == dim else 1 for axis in range(len(dims))])
    return loudness


def noise(own_key, extent, deviation, limit, cuts=(), kind=jnp.bfloat16):
    gain = levels(own_key, extent, cuts, -0.22, 0.18) if cuts else 1.0
    drawn = jax.random.normal(own_key, extent, jnp.float32) * deviation * gain
    return jnp.minimum(jnp.maximum(drawn, -limit), limit).astype(kind)


def setup_inputs(seed: int = 0) -> dict:
    arg_keys = jax.random.split(jax.random.key(seed), 4)
    parent_front = draw_parent_front(jax.random.fold_in(arg_keys[3], 71), 0)
    child_tiles = noise(arg_keys[1], (DEVICES, STORED, TILE, TILE), 1.0, 6.0, ((0, 32),))
    tile_target = draw_tile_target(jax.random.fold_in(arg_keys[3], 71), 0)
    return {"parent_front": parent_front, "child_tiles": child_tiles, "tile_target": tile_target}


def reference(parent_front, child_tiles, tile_target):
    tiles = parent_front.reshape(PTILES, TILE, PTILES, TILE)
    rows = tile_target[:, :, 0].reshape(-1)
    cols = tile_target[:, :, 1].reshape(-1)
    addend = child_tiles.reshape(-1, TILE, TILE).astype(jnp.float32)
    tiles = tiles.at[rows, :, cols, :].add(addend)
    front = tiles.reshape(FRONT, FRONT)
    for step in range(PANELS):
        start = step * TILE
        end = start + TILE
        lower = jnp.linalg.cholesky(front[start:end, start:end])
        panel = front[end:, start:end]
        solved = jax.scipy.linalg.solve_triangular(lower, panel.T, lower=True).T
        trailing = front[end:, end:] - jnp.dot(solved, solved.T, precision=lax.Precision.HIGHEST)
        front = front.at[start:end, start:end].set(lower)
        front = front.at[end:, start:end].set(solved)
        front = front.at[start:end, end:].set(jnp.zeros((TILE, FRONT - end), jnp.float32))
        front = front.at[end:, end:].set(trailing)
    return front.reshape(LROWS, N_ROW, TILE, LCOLS, N_COL, TILE)
```

```python
import jax
import jax.numpy as jnp
from jax import lax
from jax.sharding import PartitionSpec as P

PANELS = 6
HIGH = lax.Precision.HIGH


def dot(a, b):
    return jnp.dot(a, b, precision=HIGH)


def dot_t(a, b):
    return lax.dot_general(a, b, (((1,), (1,)), ((), ())), precision=HIGH)


def lower_inverse(lower):
    size = lower.shape[0]
    eye = jnp.eye(size, dtype=jnp.float32)
    inv_diag = 1.0 / jnp.sum(lower * eye, axis=0)
    power = eye - lower * inv_diag[None, :]
    result = eye + power
    reach = 2
    while reach < size:
        power = dot(power, power)
        result = result + dot(result, power)
        reach *= 2
    return result * inv_diag[:, None]


def leading_factor(first, row_count, col_count, my_row, my_col):
    tile = first.shape[1]
    grid = lax.all_gather(first[0], ("row", "col"), axis=0)
    grid = grid.reshape(row_count, col_count, tile, tile)
    pairs = [(i, j) for j in range(row_count, PANELS) for i in range(j, PANELS)]
    extra = {}
    if pairs:
        mine = [
            jnp.where(
                (my_row == i % row_count) & (my_col == j),
                first[i // row_count],
                jnp.zeros((), jnp.float32),
            )
            for i, j in pairs
        ]
        summed = lax.psum(jnp.stack(mine), ("row", "col"))
        extra = {pair: summed[n] for n, pair in enumerate(pairs)}

    def tile_at(i, j):
        if i < row_count:
            return grid[i, j]
        if j < row_count:
            return grid[j, i].T
        return extra[i, j]

    lead = {}
    inverses = []
    below = None
    for k in range(PANELS):
        column = jnp.concatenate([tile_at(i, k) for i in range(k, PANELS)], axis=0)
        if k:
            left = jnp.concatenate(
                [jnp.concatenate([lead[i, j] for j in range(k)], axis=1) for i in range(k, PANELS)], axis=0
            )
            column = column - dot_t(left, left[:tile])
        pivot = column[:tile]
        lower = jnp.linalg.cholesky(pivot)
        inverse = lower_inverse(lower)
        inverses.append(inverse)
        lead[k, k] = lower
        if k + 1 < PANELS:
            below = dot_t(column[tile:], inverse)
            for i in range(k + 1, PANELS):
                lead[i, k] = below[(i - k - 1) * tile:(i - k) * tile]
    return lead, inverses


def shards(parent_front, child_tiles, tile_target):
    lrows = parent_front.shape[0]
    tile = parent_front.shape[2]
    lcols = parent_front.shape[3]
    row_count = lax.axis_size("row")
    col_count = lax.axis_size("col")
    devices = row_count * col_count
    my_row = lax.axis_index("row")
    my_col = lax.axis_index("col")
    myself = my_row * col_count + my_col
    front = parent_front.reshape(lrows, tile, lcols, tile)
    first = PANELS // row_count
    lead_rows = -(-PANELS // row_count)

    lead, inverses = leading_factor(front[:lead_rows, :, 0, :], row_count, col_count, my_row, my_col)

    stored = child_tiles.shape[1]
    held = child_tiles.reshape(stored, tile, tile)
    rows_all = tile_target[:, :, 0]
    cols_all = tile_target[:, :, 1]
    owner_all = rows_all % row_count * col_count + cols_all % col_count
    local_all = rows_all // row_count * lcols + cols_all // col_count
    peers = jnp.arange(devices, dtype=jnp.int32)
    my_owner = lax.dynamic_index_in_dim(owner_all, myself, 0, keepdims=False)
    sending = my_owner[None, :] == peers[:, None]
    present = jnp.any(sending, axis=1)
    picked = jnp.sum(jnp.where(sending, jnp.arange(stored, dtype=jnp.int32)[None, :], 0), axis=1)
    outgoing = jnp.where(present[:, None, None], held[picked], jnp.zeros((), jnp.bfloat16))
    arrived = lax.all_to_all(outgoing, ("row", "col"), split_axis=0, concat_axis=0, tiled=True)
    landing = owner_all == myself
    came = jnp.any(landing, axis=1)
    where_to = jnp.sum(jnp.where(landing, local_all, 0), axis=1)
    slots = jnp.arange(lrows * lcols, dtype=jnp.int32)
    onehot = ((where_to[:, None] == slots[None, :]) & came[:, None]).astype(jnp.bfloat16)
    onehot = onehot.reshape(devices, lrows, lcols)[:, first:]
    summed = jnp.einsum("dij,dxy->ijxy", onehot, arrived, preferred_element_type=jnp.float32)
    lower_front = front[first:].transpose(0, 2, 1, 3) + summed
    count = lrows - first

    panel = lax.all_gather(lower_front[:, 0], "col", axis=0)[:PANELS]
    pick = my_col // row_count + col_count // row_count * jnp.arange(lcols, dtype=jnp.int32) - first
    chosen = panel[:, jnp.clip(pick, 0, count - 1)]
    root = my_row == my_col % row_count
    chosen = lax.psum(jnp.where(root, chosen, jnp.zeros((), jnp.float32)), "row")
    stack = jnp.concatenate([panel, chosen], axis=1).reshape(PANELS, (count + lcols) * tile, tile)
    solved = []
    for k in range(PANELS):
        value = stack[k]
        if k:
            row = jnp.concatenate([lead[k, j] for j in range(k)], axis=1)
            value = value - dot_t(jnp.concatenate(solved, axis=1), row)
        solved.append(dot_t(value, inverses[k]))
    wide = jnp.concatenate(solved, axis=1)
    update = dot_t(wide[:count * tile], wide[count * tile:])
    update = update.reshape(count, tile, lcols, tile)
    row_ids = my_row + row_count * jnp.arange(lrows, dtype=jnp.int32)
    col_ids = my_col + col_count * jnp.arange(lcols, dtype=jnp.int32)
    trailing = lower_front.transpose(0, 2, 1, 3) - update
    at = jnp.minimum(my_col, PANELS - 1)
    mine = lax.dynamic_index_in_dim(
        wide[:count * tile].reshape(count, tile, PANELS, tile), at, 2, keepdims=True
    )
    in_panel = (col_ids < PANELS)[None, None, :, None]
    below = jnp.where(in_panel, mine, trailing)
    zero = jnp.zeros((tile, tile), jnp.float32)
    grid = jnp.stack([jnp.stack([lead.get((i, j), zero) for j in range(PANELS)]) for i in range(PANELS)])
    tops = []
    for i in range(lead_rows):
        picked_tile = grid[jnp.minimum(my_row + row_count * i, PANELS - 1), at]
        tops.append(jnp.where((col_ids < PANELS)[None, :, None], picked_tile[:, None, :], 0.0))
    out = []
    for i in range(lrows):
        if i < first:
            out.append(tops[i])
        elif i < lead_rows:
            out.append(jnp.where(row_ids[i] < PANELS, tops[i], below[i - first]))
        else:
            out.append(below[i - first])
    return jnp.stack(out).reshape(parent_front.shape)


def solution(mesh):
    return jax.shard_map(
        shards,
        mesh=mesh,
        in_specs=(
            P(None, "row", None, None, "col", None),
            P(("row", "col"), None, None, None),
            P(),
        ),
        out_specs=P(None, "row", None, None, "col", None),
        check_vma=False,
    )
```

```python
import jax
import jax.numpy as jnp
from jax import lax
from jax.sharding import PartitionSpec as P

PANELS = 6
HIGH = lax.Precision.HIGH


def dot(a, b):
    return jnp.dot(a, b, precision=HIGH)


def dot_t(a, b):
    return lax.dot_general(a, b, (((1,), (1,)), ((), ())), precision=HIGH)


def lower_inverse(lower):
    size = lower.shape[0]
    eye = jnp.eye(size, dtype=jnp.float32)
    inv_diag = 1.0 / jnp.sum(lower * eye, axis=0)
    power = eye - lower * inv_diag[None, :]
    result = eye + power
    power = dot(power, power)
    reach = 2
    while 2 * reach < size:
        both = dot(jnp.concatenate([result, power], axis=0), power)
        result = result + both[:size]
        power = both[size:]
        reach *= 2
    result = result + dot(result, power)
    return result * inv_diag[:, None]


def tile_factor(pivot):
    half = pivot.shape[0] // 2
    low1 = lax.linalg.cholesky(pivot[:half, :half], symmetrize_input=False)
    inv1 = lower_inverse(low1)
    below = dot_t(pivot[half:, :half], inv1)
    low2 = lax.linalg.cholesky(pivot[half:, half:] - dot_t(below, below), symmetrize_input=False)
    inv2 = lower_inverse(low2)
    zero = jnp.zeros((half, half), jnp.float32)
    corner = -dot(inv2, dot(below, inv1))
    lower = jnp.block([[low1, zero], [below, low2]])
    inverse = jnp.block([[inv1, zero], [corner, inv2]])
    return lower, inverse


def leading_factor(first, extra, row_count, col_count):
    tile = first.shape[0]
    grid = lax.all_gather(first, ("row", "col"), axis=0)
    grid = grid.reshape(row_count, col_count, tile, tile)
    pairs = [(i, j) for j in range(row_count, PANELS) for i in range(j, PANELS)]
    def tile_at(i, j):
        if i < row_count:
            return grid[i, j]
        if j < row_count:
            return grid[j, i].T
        return extra[i, j]

    lead = {}
    inverses = []
    below = None
    for k in range(PANELS):
        column = jnp.concatenate([tile_at(i, k) for i in range(k, PANELS)], axis=0)
        if k:
            left = jnp.concatenate(
                [jnp.concatenate([lead[i, j] for j in range(k)], axis=1) for i in range(k, PANELS)], axis=0
            )
            column = column - dot_t(left, left[:tile])
        pivot = column[:tile]
        lower, inverse = tile_factor(pivot)
        inverses.append(inverse)
        lead[k, k] = lower
        if k + 1 < PANELS:
            below = dot_t(column[tile:], inverse)
            for i in range(k + 1, PANELS):
                lead[i, k] = below[(i - k - 1) * tile:(i - k) * tile]
    return lead, inverses


def shards(parent_front, child_tiles, tile_target):
    lrows = parent_front.shape[0]
    tile = parent_front.shape[2]
    lcols = parent_front.shape[3]
    row_count = lax.axis_size("row")
    col_count = lax.axis_size("col")
    devices = row_count * col_count
    my_row = lax.axis_index("row")
    my_col = lax.axis_index("col")
    myself = my_row * col_count + my_col
    front = parent_front.reshape(lrows, tile, lcols, tile)
    first = PANELS // row_count
    lead_rows = -(-PANELS // row_count)

    stored = child_tiles.shape[1]
    held = child_tiles.reshape(stored, tile, tile)
    rows_all = tile_target[:, :, 0]
    cols_all = tile_target[:, :, 1]
    owner_all = rows_all % row_count * col_count + cols_all % col_count
    local_all = rows_all // row_count * lcols + cols_all // col_count
    peers = jnp.arange(devices, dtype=jnp.int32)
    my_owner = lax.dynamic_index_in_dim(owner_all, myself, 0, keepdims=False)
    sending = my_owner[None, :] == peers[:, None]
    present = jnp.any(sending, axis=1)
    picked = jnp.sum(jnp.where(sending, jnp.arange(stored, dtype=jnp.int32)[None, :], 0), axis=1)
    outgoing = jnp.where(present[:, None, None], held[picked], jnp.zeros((), jnp.bfloat16))
    arrived = lax.all_to_all(outgoing, ("row", "col"), split_axis=0, concat_axis=0, tiled=True)
    landing = owner_all == myself
    came = jnp.any(landing, axis=1)
    where_to = jnp.sum(jnp.where(landing, local_all, 0), axis=1)
    slots = jnp.arange(lrows * lcols, dtype=jnp.int32)
    onehot = ((where_to[:, None] == slots[None, :]) & came[:, None]).astype(jnp.bfloat16)
    onehot = onehot.reshape(devices, lrows, lcols)[:, first:]
    summed = jnp.einsum("dij,dxy->ijxy", onehot, arrived, preferred_element_type=jnp.float32)
    lower_front = front[first:].transpose(0, 2, 1, 3) + summed
    count = lrows - first

    panel = lax.all_gather(lower_front[:, 0], "col", axis=0)[:PANELS]
    pick = my_col // row_count + col_count // row_count * jnp.arange(lcols, dtype=jnp.int32) - first
    source = panel[:, jnp.clip(pick, 0, count - 1)]
    root = my_row == my_col % row_count
    parts = []
    for j in range(lcols):
        own = source[:, j]
        total = jnp.where(root, own, 0.0)
        for shift in range(1, row_count):
            pairs = [
                (c % row_count * col_count + c, (c + shift) % row_count * col_count + c)
                for c in range(col_count)
                if c + j * col_count >= PANELS
            ]
            total = total + lax.ppermute(own, ("row", "col"), pairs)
        parts.append(total)
    chosen = jnp.stack(parts, axis=1)

    extra = {}
    if PANELS > row_count:
        corner = panel[row_count:, 0]
        holders = PANELS - row_count
        received = [corner] + [
            lax.ppermute(corner, "row", [(r, (r + shift) % row_count) for r in range(holders)])
            for shift in range(1, row_count)
        ]
        for r in range(holders):
            full = received[0]
            for shift in range(1, row_count):
                full = jnp.where((my_row - r) % row_count == shift, received[shift], full)
            for j in range(r + 1):
                extra[row_count + r, row_count + j] = full[j]
    lead, inverses = leading_factor(front[0, :, 0, :], extra, row_count, col_count)

    stack = jnp.concatenate([panel, chosen], axis=1).reshape(PANELS, (count + lcols) * tile, tile)
    solved = []
    for k in range(PANELS):
        value = stack[k]
        if k:
            row = jnp.concatenate([lead[k, j] for j in range(k)], axis=1)
            value = value - dot_t(jnp.concatenate(solved, axis=1), row)
        solved.append(dot_t(value, inverses[k]))
    wide = jnp.concatenate(solved, axis=1)
    update = dot_t(wide[:count * tile], wide[count * tile:])
    update = update.reshape(count, tile, lcols, tile)
    row_ids = my_row + row_count * jnp.arange(lrows, dtype=jnp.int32)
    col_ids = my_col + col_count * jnp.arange(lcols, dtype=jnp.int32)
    trailing = lower_front.transpose(0, 2, 1, 3) - update
    at = jnp.minimum(my_col, PANELS - 1)
    mine = lax.dynamic_index_in_dim(
        wide[:count * tile].reshape(count, tile, PANELS, tile), at, 2, keepdims=True
    )
    in_panel = (col_ids < PANELS)[None, None, :, None]
    below = jnp.where(in_panel, mine, trailing)
    zero = jnp.zeros((tile, tile), jnp.float32)
    grid = jnp.stack([jnp.stack([lead.get((i, j), zero) for j in range(PANELS)]) for i in range(PANELS)])
    tops = []
    for i in range(lead_rows):
        picked_tile = grid[jnp.minimum(my_row + row_count * i, PANELS - 1), at]
        tops.append(jnp.where((col_ids < PANELS)[None, :, None], picked_tile[:, None, :], 0.0))
    out = []
    for i in range(lrows):
        if i < first:
            out.append(tops[i])
        elif i < lead_rows:
            out.append(jnp.where(row_ids[i] < PANELS, tops[i], below[i - first]))
        else:
            out.append(below[i - first])
    return jnp.stack(out).reshape(parent_front.shape)


def solution(mesh):
    return jax.shard_map(
        shards,
        mesh=mesh,
        in_specs=(
            P(None, "row", None, None, "col", None),
            P(("row", "col"), None, None, None),
            P(),
        ),
        out_specs=P(None, "row", None, None, "col", None),
        check_vma=False,
    )
```

```python
import jax
import jax.numpy as jnp
from jax import lax
from jax.sharding import PartitionSpec as P

PANELS = 6
HIGH = lax.Precision.HIGH


def dot(a, b):
    return jnp.dot(a, b, precision=HIGH)


def dot_t(a, b):
    return lax.dot_general(a, b, (((1,), (1,)), ((), ())), precision=HIGH)


def lower_inverse(lower):
    size = lower.shape[0]
    eye = jnp.eye(size, dtype=jnp.float32)
    inv_diag = 1.0 / jnp.sum(lower * eye, axis=0)
    power = eye - lower * inv_diag[None, :]
    result = eye + power
    power = dot(power, power)
    reach = 2
    while 2 * reach < size:
        both = dot(jnp.concatenate([result, power], axis=0), power)
        result = result + both[:size]
        power = both[size:]
        reach *= 2
    result = result + dot(result, power)
    return result * inv_diag[:, None]


def tile_factor(pivot):
    half = pivot.shape[0] // 2
    low1 = lax.linalg.cholesky(pivot[:half, :half], symmetrize_input=False)
    inv1 = lower_inverse(low1)
    below = dot_t(pivot[half:, :half], inv1)
    low2 = lax.linalg.cholesky(pivot[half:, half:] - dot_t(below, below), symmetrize_input=False)
    inv2 = lower_inverse(low2)
    zero = jnp.zeros((half, half), jnp.float32)
    corner = -dot(inv2, dot(below, inv1))
    lower = jnp.block([[low1, zero], [below, low2]])
    inverse = jnp.block([[inv1, zero], [corner, inv2]])
    return lower, inverse


def leading_steps(grid, extra, lead, inverses, start, stop):
    row_count, _, tile, _ = grid.shape

    def tile_at(i, j):
        if i < row_count:
            return grid[i, j]
        if j < row_count:
            return grid[j, i].T
        return extra[i, j]

    for k in range(start, stop):
        column = jnp.concatenate([tile_at(i, k) for i in range(k, PANELS)], axis=0)
        if k:
            left = jnp.concatenate(
                [jnp.concatenate([lead[i, j] for j in range(k)], axis=1) for i in range(k, PANELS)], axis=0
            )
            column = column - dot_t(left, left[:tile])
        pivot = column[:tile]
        lower, inverse = tile_factor(pivot)
        inverses.append(inverse)
        lead[k, k] = lower
        if k + 1 < PANELS:
            below = dot_t(column[tile:], inverse)
            for i in range(k + 1, PANELS):
                lead[i, k] = below[(i - k - 1) * tile:(i - k) * tile]


def shards(parent_front, child_tiles, tile_target):
    lrows = parent_front.shape[0]
    tile = parent_front.shape[2]
    lcols = parent_front.shape[3]
    row_count = lax.axis_size("row")
    col_count = lax.axis_size("col")
    devices = row_count * col_count
    my_row = lax.axis_index("row")
    my_col = lax.axis_index("col")
    myself = my_row * col_count + my_col
    front = parent_front.reshape(lrows, tile, lcols, tile)
    first = PANELS // row_count
    lead_rows = -(-PANELS // row_count)

    stored = child_tiles.shape[1]
    held = child_tiles.reshape(stored, tile, tile)
    rows_all = tile_target[:, :, 0]
    cols_all = tile_target[:, :, 1]
    owner_all = rows_all % row_count * col_count + cols_all % col_count
    local_all = rows_all // row_count * lcols + cols_all // col_count
    peers = jnp.arange(devices, dtype=jnp.int32)
    my_owner = lax.dynamic_index_in_dim(owner_all, myself, 0, keepdims=False)
    sending = my_owner[None, :] == peers[:, None]
    present = jnp.any(sending, axis=1)
    picked = jnp.sum(jnp.where(sending, jnp.arange(stored, dtype=jnp.int32)[None, :], 0), axis=1)
    outgoing = jnp.where(present[:, None, None], held[picked], jnp.zeros((), jnp.bfloat16))
    grid = lax.all_gather(front[0, :, 0, :], ("row", "col"), axis=0)
    grid, outgoing = lax.optimization_barrier((grid, outgoing))
    grid = grid.reshape(row_count, col_count, tile, tile)
    arrived = lax.all_to_all(outgoing, ("row", "col"), split_axis=0, concat_axis=0, tiled=True)
    lead = {}
    inverses = []
    extra = {}
    leading_steps(grid, extra, lead, inverses, 0, 2)
    arrived, inverses[1] = lax.optimization_barrier((arrived, inverses[1]))
    landing = owner_all == myself
    came = jnp.any(landing, axis=1)
    where_to = jnp.sum(jnp.where(landing, local_all, 0), axis=1)
    slots = jnp.arange(lrows * lcols, dtype=jnp.int32)
    onehot = ((where_to[:, None] == slots[None, :]) & came[:, None]).astype(jnp.bfloat16)
    onehot = onehot.reshape(devices, lrows, lcols)[:, first:]
    summed = jnp.einsum("dij,dxy->ijxy", onehot, arrived, preferred_element_type=jnp.float32)
    lower_front = front[first:].transpose(0, 2, 1, 3) + summed
    count = lrows - first

    panel = lax.all_gather(lower_front[:, 0], "col", axis=0)[:PANELS]
    pick = my_col // row_count + col_count // row_count * jnp.arange(lcols, dtype=jnp.int32) - first
    source = panel[:, jnp.clip(pick, 0, count - 1)]
    root = my_row == my_col % row_count
    parts = []
    for j in range(lcols):
        own = source[:, j]
        total = jnp.where(root, own, 0.0)
        for shift in range(1, row_count):
            pairs = [
                (c % row_count * col_count + c, (c + shift) % row_count * col_count + c)
                for c in range(col_count)
                if c + j * col_count >= PANELS
            ]
            total = total + lax.ppermute(own, ("row", "col"), pairs)
        parts.append(total)
    chosen = jnp.stack(parts, axis=1)

    if PANELS > row_count:
        corner = panel[row_count:, 0]
        holders = PANELS - row_count
        received = [corner] + [
            lax.ppermute(corner, "row", [(r, (r + shift) % row_count) for r in range(holders)])
            for shift in range(1, row_count)
        ]
        for r in range(holders):
            full = received[0]
            for shift in range(1, row_count):
                full = jnp.where((my_row - r) % row_count == shift, received[shift], full)
            for j in range(r + 1):
                extra[row_count + r, row_count + j] = full[j]
    leading_steps(grid, extra, lead, inverses, 2, PANELS)

    stack = jnp.concatenate([panel, chosen], axis=1).reshape(PANELS, (count + lcols) * tile, tile)
    solved = []
    for k in range(PANELS):
        value = stack[k]
        if k:
            row = jnp.concatenate([lead[k, j] for j in range(k)], axis=1)
            value = value - dot_t(jnp.concatenate(solved, axis=1), row)
        solved.append(dot_t(value, inverses[k]))
    wide = jnp.concatenate(solved, axis=1)
    update = dot_t(wide[:count * tile], wide[count * tile:])
    update = update.reshape(count, tile, lcols, tile)
    row_ids = my_row + row_count * jnp.arange(lrows, dtype=jnp.int32)
    col_ids = my_col + col_count * jnp.arange(lcols, dtype=jnp.int32)
    trailing = lower_front.transpose(0, 2, 1, 3) - update
    at = jnp.minimum(my_col, PANELS - 1)
    mine = lax.dynamic_index_in_dim(
        wide[:count * tile].reshape(count, tile, PANELS, tile), at, 2, keepdims=True
    )
    in_panel = (col_ids < PANELS)[None, None, :, None]
    below = jnp.where(in_panel, mine, trailing)
    zero = jnp.zeros((tile, tile), jnp.float32)
    factor = jnp.stack([jnp.stack([lead.get((i, j), zero) for j in range(PANELS)]) for i in range(PANELS)])
    tops = []
    for i in range(lead_rows):
        picked_tile = factor[jnp.minimum(my_row + row_count * i, PANELS - 1), at]
        tops.append(jnp.where((col_ids < PANELS)[None, :, None], picked_tile[:, None, :], 0.0))
    out = []
    for i in range(lrows):
        if i < first:
            out.append(tops[i])
        elif i < lead_rows:
            out.append(jnp.where(row_ids[i] < PANELS, tops[i], below[i - first]))
        else:
            out.append(below[i - first])
    return jnp.stack(out).reshape(parent_front.shape)


def solution(mesh):
    return jax.shard_map(
        shards,
        mesh=mesh,
        in_specs=(
            P(None, "row", None, None, "col", None),
            P(("row", "col"), None, None, None),
            P(),
        ),
        out_specs=P(None, "row", None, None, "col", None),
        check_vma=False,
    )
```
